32 devices in a mesh: groups: 2 (over x), expert: 16 (over z, y, core).
Axes of the slice: x: 2, y: 2, z: 4, core: 2. Of those that a mesh axis runs over, the one named last changes fastest.
Arguments:
- hidden_states: bfloat16 [2, 1024, 2560], P(None, ('groups', 'expert')), parts along dimension 1, may hold values from -6 to 6
- route_ids: int32 [2, 1024, 8], P(None, ('groups', 'expert')), parts along dimension 1, may hold values from 0 to 15, all different within a row; in each aligned block of 32 rows (0 to 31, 32 to 63, ..., all dimensions but the last counted through in order) at most 24 rows name the same one
- route_weights: float32 [2, 1024, 8], P(None, ('groups', 'expert')), parts along dimension 1, may hold values from 0.05 to 1
- gate_proj: bfloat16 [16, 2560, 768], P('expert'), may hold values from -0.125 to 0.125
- up_proj: bfloat16 [16, 2560, 768], P('expert'), may hold values from -0.125 to 0.125
- down_proj: bfloat16 [16, 768, 2560], P('expert'), may hold values from -0.21875 to 0.21875
Outputs:
- moe_output: bfloat16 [2, 1024, 2560], P(None, ('groups', 'expert')), parts along dimension 1
The draws below stay inside these ranges and needn't reach their ends.
There are 2 independent parts, one for each index of `groups`. The reference program is written for one: setup_inputs(seed, part) draws one part's arguments, and reference() takes and returns one part's arrays. A program takes and returns all parts, laid end to end along the dimension named above; an argument that names none is the same for every part. Nothing has to cross between parts.
Inputs may be any that keep to these rules, and one draw needn't show every extreme that they name: `route_ids`: each row names 8 different experts. In each micro-batch, the 32 rows of one device name one expert at most 24 times, and some device names some expert exactly 24 times.
All inputs are finite; a program needn't handle non-finite values.
Results may differ from the reference program's by a relative error of at most 0.0057.
Values may be sent and summed in bfloat16 or wider, within the bound.
No kernel may reach another device: no remote copies, remote signals or barrier semaphores. Data moves between devices by JAX's collectives and lax.ppermute only.
A program may use at most 64 MiB of HBM per device.

```python
import math
import jax
import jax.numpy as jnp
import numpy as np
from jax import lax

D = 2560
FF = 768
TOPK = 8
STEPS = 2
ROWS = 32
EXPERTS = 16
TOKENS = 512
CAP = 24
N_EXPERT = 16


def level_of(own_key, dims, cuts, smallest, largest):
    def one(dim, parts):
        heights = jax.random.uniform(jax.random.fold_in(jax.random.fold_in(own_key, 6), dim), (parts,), jnp.float32, smallest / len(cuts), largest / len(cuts))
        return jnp.repeat(jnp.exp(heights), dims[dim] // parts).reshape((-1,) + (1,) * (len(dims) - dim - 1))

    factor_of = one(*cuts[0])
    for cut in cuts[1:]:
        factor_of = factor_of * one(*cut)
    return factor_of


def routed_block(key, own, number, rows, amount, top, limit, lean):
    sequence = jax.random.permutation(key, amount)
    packed, ordinary = shares(amount, rows * top, limit, lean, True), shares(amount, rows * top, limit, lean, False)
    places = jnp.arange(amount)

    def named(tallies, offset_by):
        used = int((tallies > 0).sum())
        fixed = max(1, used // 4)
        shifted = fixed + (places - fixed + offset_by * (used - fixed)) % max(1, amount - fixed)
        return jnp.zeros((amount,), jnp.int32).at[sequence[jnp.where(places < fixed, places, shifted)]].set(jnp.asarray(tallies, jnp.int32))

    tallies = jnp.where(number % 4 == 0, named(packed, number // 4), named(ordinary, number - number // 4 - 1))
    mixed = jax.random.permutation(jax.random.fold_in(own, 3), amount)
    donor, receiver = mixed[0:amount // 2 * 2:2], mixed[1:amount // 2 * 2:2]
    room = jnp.minimum(tallies[donor] - 1, limit - tallies[receiver]) // 2
    room = jnp.where((donor == sequence[0]) | (receiver == sequence[0]) | (tallies[receiver] == 0), 0, jnp.maximum(room, 0))
    shifted = jax.random.randint(jax.random.fold_in(own, 4), (amount // 2,), 0, 1 << 20) % (room + 1)
    tallies = tallies.at[donor].add(-shifted).at[receiver].add(shifted)
    items = jnp.searchsorted(jnp.cumsum(tallies), jnp.arange(rows * top), side="right").astype(jnp.int32)
    table = items.reshape(top, rows).T
    table = table[jax.random.permutation(jax.random.fold_in(own, 1), rows)]
    offset_by = jax.random.randint(jax.random.fold_in(own, 2), (rows, 1), 0, top)
    return jnp.take_along_axis(table, (jnp.arange(top)[None, :] + offset_by) % top, axis=1)


def shares(number_of, total, limit, skew, full):
    portions = [(1 << 20) // math.isqrt(standing ** skew) + 1 for standing in range(1, number_of + 1)]
    largest = limit if full else min(limit, max(-(-total // number_of), total * portions[0] // sum(portions)))
    least = 1 if total - largest >= number_of - 1 else 0
    given, rest = [largest] + [least] * (number_of - 1), total - largest - least * (number_of - 1)
    while rest > 0:
        candidates = [i for i in range(1, number_of) if given[i] < largest] or [i for i in range(1, number_of) if given[i] < limit]
        pool, left = sum([portions[i] for i in candidates]), rest
        for i in candidates:
            extra = min(limit - given[i], max(1, left * portions[i] // pool), rest)
            given[i] = given[i] + extra
            rest = rest - extra
    return np.array(given)


def scatter_about(rng, extent, deviation, most, split=(), dtype=jnp.bfloat16):
    entries = deviation * jax.random.normal(rng, extent, jnp.float32)
    if split:
        entries = entries * level_of(rng, extent, split, -0.22, 0.18)
    return jnp.clip(entries, -most, most).astype(dtype)


def setup_inputs(seed: int = 0, part: int = 0) -> dict:
    keys = jax.random.split(jax.random.key(seed), 7)
    part_keys = jax.random.split(jax.random.fold_in(keys[6], part), 7)
    hidden_states = scatter_about(part_keys[0], (STEPS, TOKENS, D), 1.0, 6.0, ((1, 16),))
    route_ids_keys = jax.random.split(jax.random.fold_in(part_keys[1], 1), STEPS * TOKENS // ROWS)
    route_ids_turns = jax.random.permutation(jax.random.fold_in(part_keys[1], 3), STEPS * TOKENS // ROWS)
    route_ids = jax.vmap(lambda own, number: routed_block(jax.random.fold_in(part_keys[1], 2), own, number, ROWS, EXPERTS, TOPK, CAP, 2))(route_ids_keys, route_ids_turns).reshape((STEPS, TOKENS, TOPK))
    route_weights = jnp.clip(0.05 + 0.95 * jax.random.uniform(part_keys[2], (STEPS, TOKENS, TOPK), jnp.float32) ** level_of(part_keys[2], (STEPS, TOKENS, TOPK), ((1, 16),), -0.2, 0.2), 0.05, 1.0)
    gate_proj = scatter_about(keys[3], (EXPERTS, D, FF), D ** -0.5, 0.125, ((0, 16),))
    up_proj = scatter_about(keys[4], (EXPERTS, D, FF), D ** -0.5, 0.125, ((0, 16),))
    down_proj = scatter_about(keys[5], (EXPERTS, FF, D), FF ** -0.5, 0.21875, ((0, 16),))
    return dict(hidden_states=hidden_states, route_ids=route_ids, route_weights=route_weights, gate_proj=gate_proj, up_proj=up_proj, down_proj=down_proj)


def slot_targets(route_row, capacity):
    labels = lax.broadcasted_iota(jnp.int32, (TOKENS, TOPK, EXPERTS), 2)
    onehot = (route_row[:, :, None] == labels).astype(jnp.int32)
    per_row = jnp.sum(onehot, axis=1)
    before = jnp.cumsum(per_row, axis=0) - per_row
    position = jnp.sum(onehot * before[:, None, :], axis=2)
    return (route_row * capacity + position).astype(jnp.int32)


def apply_expert(operands):
    expert_rows, gate_weight, up_weight, down_weight = operands
    gate_values = jnp.dot(expert_rows, gate_weight, preferred_element_type=jnp.float32)
    up_values = jnp.dot(expert_rows, up_weight, preferred_element_type=jnp.float32)
    hidden = (jax.nn.silu(gate_values) * up_values).astype(jnp.bfloat16)
    return jnp.dot(hidden, down_weight, preferred_element_type=jnp.float32).astype(jnp.bfloat16)


def reference(hidden_states, route_ids, route_weights, gate_proj, up_proj, down_proj):
    capacity = N_EXPERT * CAP
    outputs = []
    for step_index in range(STEPS):
        targets = slot_targets(route_ids[step_index], capacity).reshape(-1)
        sources = jnp.repeat(hidden_states[step_index], TOPK, axis=0)
        buffer = jnp.zeros((EXPERTS * capacity, D), jnp.bfloat16).at[targets].set(sources)
        results = lax.map(apply_expert, (buffer.reshape(EXPERTS, capacity, D), gate_proj, up_proj, down_proj))
        gathered = results.reshape(EXPERTS * capacity, D)[targets].reshape(TOKENS, TOPK, D)
        weights = route_weights[step_index]
        normalized = weights / jnp.sum(weights, axis=1, keepdims=True)
        combined = jnp.sum(gathered.astype(jnp.float32) * normalized[:, :, None], axis=1)
        outputs.append(combined.astype(jnp.bfloat16))
    return jnp.stack(outputs)
```

```python
import jax
import jax.numpy as jnp
from jax import lax
from jax.sharding import PartitionSpec as P

PIECES = 4


def swap(array, axis_size, bit):
    return lax.ppermute(array, "expert", [(i, i ^ bit) for i in range(axis_size)])


def dense_weights(route_ids, route_weights, experts):
    normalized = route_weights / jnp.sum(route_weights, axis=1, keepdims=True)
    labels = lax.broadcasted_iota(jnp.int32, (*route_ids.shape, experts), 2)
    chosen = jnp.where(route_ids[:, :, None] == labels, normalized[:, :, None], 0.0)
    return jnp.sum(chosen, axis=1)


def with_weights(rows, weights):
    high = weights.astype(jnp.bfloat16)
    low = (weights - high.astype(jnp.float32)).astype(jnp.bfloat16)
    experts = weights.shape[1]
    fill = -2 * experts % 128
    return jnp.concatenate(
        [rows, high, low, jnp.zeros((rows.shape[0], fill), jnp.bfloat16)], axis=1
    )


def expert_rows(rows, experts, gate_proj, up_proj, down_proj):
    width = gate_proj.shape[0]
    own = lax.axis_index("expert")
    tokens = rows[:, :width]
    spread = rows[:, width : width + 2 * experts].astype(jnp.float32)
    lane = lax.broadcasted_iota(jnp.int32, spread.shape, 1)
    weight = jnp.sum(jnp.where(lane % experts == own, spread, 0.0), axis=1, keepdims=True)
    gate_values = jnp.dot(tokens, gate_proj, preferred_element_type=jnp.float32)
    up_values = jnp.dot(tokens, up_proj, preferred_element_type=jnp.float32)
    hidden = (jax.nn.silu(gate_values) * up_values).astype(jnp.bfloat16)
    result = jnp.dot(hidden, down_proj, preferred_element_type=jnp.float32)
    return (result * weight).astype(jnp.bfloat16)


def on_device(hidden_states, route_ids, route_weights, gate_proj, up_proj, down_proj):
    step_count, row_count, feature_width = hidden_states.shape
    axis_size = lax.axis_size("expert")
    experts = axis_size * gate_proj.shape[0]
    total = step_count * row_count
    share = total // PIECES
    bits = [1 << i for i in reversed(range(axis_size.bit_length() - 1))]
    weights = dense_weights(
        route_ids.reshape(total, -1), route_weights.reshape(total, -1), experts
    )
    rows = with_weights(hidden_states.reshape(total, feature_width), weights)
    outputs = []
    for piece in range(PIECES):
        held = rows[piece * share : (piece + 1) * share]
        for bit in bits:
            held = jnp.concatenate([held, swap(held, axis_size, bit)], axis=0)
        sums = expert_rows(held, experts, gate_proj[0], up_proj[0], down_proj[0])
        for bit in reversed(bits):
            half = sums.shape[0] // 2
            arrived = swap(sums[half:], axis_size, bit)
            sums = (
                sums[:half].astype(jnp.float32) + arrived.astype(jnp.float32)
            ).astype(jnp.bfloat16)
        outputs.append(sums)
    return jnp.concatenate(outputs, axis=0).reshape(hidden_states.shape)


def solution(mesh):
    placed = (
        P(None, ("groups", "expert"), None),
        P(None, ("groups", "expert"), None),
        P(None, ("groups", "expert"), None),
        P("expert", None, None),
        P("expert", None, None),
        P("expert", None, None),
    )
    return jax.shard_map(
        on_device,
        mesh=mesh,
        in_specs=placed,
        out_specs=P(None, ("groups", "expert"), None),
        check_vma=False,
    )
```

```python
import jax
import jax.numpy as jnp
from jax import lax
from jax.experimental import pallas as pl
from jax.experimental.pallas import tpu as pltpu
from jax.sharding import PartitionSpec as P

PIECES = 4
LANES = 128
BLOCK = 256


def swap(array, axis_size, bit):
    return lax.ppermute(array, "expert", [(i, i ^ bit) for i in range(axis_size)])


def dense_weights(route_ids, route_weights, experts):
    normalized = route_weights / jnp.sum(route_weights, axis=1, keepdims=True)
    labels = lax.broadcasted_iota(jnp.int32, (*route_ids.shape, experts), 2)
    chosen = jnp.where(route_ids[:, :, None] == labels, normalized[:, :, None], 0.0)
    return jnp.sum(chosen, axis=1)


def with_weights(rows, weights):
    high = weights.astype(jnp.bfloat16)
    low = (weights - high.astype(jnp.float32)).astype(jnp.bfloat16)
    fill = -2 * weights.shape[1] % LANES
    return jnp.concatenate(
        [rows, high, low, jnp.zeros((rows.shape[0], fill), jnp.bfloat16)], axis=1
    )


def expert_kernel(experts, own_ref, near_ref, far_ref, gate_ref, up_ref, down_ref, keep_ref, send_ref):
    width = gate_ref.shape[0]
    half = near_ref.shape[0]
    own = own_ref[0]
    block = min(BLOCK // 2, half)

    def step(index, carry):
        part = pl.ds(pl.multiple_of(index * block, block), block)
        rows = jnp.concatenate([near_ref[part, :], far_ref[part, :]], axis=0)
        tokens = rows[:, :width]
        spread = rows[:, width:].astype(jnp.float32)
        lane = lax.broadcasted_iota(jnp.int32, spread.shape, 1)
        mine = (lane == own) | (lane == own + experts)
        weight = jnp.sum(jnp.where(mine, spread, 0.0), axis=1, keepdims=True)
        gate = jnp.dot(tokens, gate_ref[...], preferred_element_type=jnp.float32)
        up = jnp.dot(tokens, up_ref[...], preferred_element_type=jnp.float32)
        hidden = (gate / (1.0 + jnp.exp(-gate)) * up).astype(jnp.bfloat16)
        result = jnp.dot(hidden, down_ref[...], preferred_element_type=jnp.float32)
        scaled = (result * weight).astype(jnp.bfloat16)
        keep_ref[part, :] = scaled[:block]
        send_ref[part, :] = scaled[block:]
        return carry

    if half == block:
        step(0, 0)
    else:
        lax.fori_loop(0, half // block, step, 0)


def expert_rows(near, far, experts, gate_proj, up_proj, down_proj):
    width, middle = gate_proj.shape
    half = near.shape[0]
    vmem = pl.BlockSpec(memory_space=pltpu.VMEM)
    shape = jax.ShapeDtypeStruct((half, width), jnp.bfloat16)
    size = 2 * half
    return pl.pallas_call(
        lambda *refs: expert_kernel(experts, *refs),
        out_shape=(shape, shape),
        in_specs=[pl.BlockSpec(memory_space=pltpu.SMEM)] + [vmem] * 5,
        out_specs=(vmem, vmem),
        compiler_params=pltpu.CompilerParams(vmem_limit_bytes=40 * 1024 * 1024),
        cost_estimate=pl.CostEstimate(
            flops=6 * size * width * middle,
            bytes_accessed=4 * size * width + 6 * width * middle,
            transcendentals=size * middle,
        ),
    )(lax.axis_index("expert").reshape(1), near, far, gate_proj, up_proj, down_proj)


def add_halves(kept, arrived):
    half = kept.shape[0] // 2
    if half == 0:
        return None

    def total(first, second):
        return (first.astype(jnp.float32) + second.astype(jnp.float32)).astype(jnp.bfloat16)

    return total(kept[:half], arrived[:half]), total(kept[half:], arrived[half:])


def on_device(hidden_states, route_ids, route_weights, gate_proj, up_proj, down_proj):
    step_count, row_count, feature_width = hidden_states.shape
    axis_size = lax.axis_size("expert")
    experts = axis_size * gate_proj.shape[0]
    total = step_count * row_count
    share = total // PIECES
    bits = [1 << i for i in reversed(range(axis_size.bit_length() - 1))]
    weights = dense_weights(
        route_ids.reshape(total, -1), route_weights.reshape(total, -1), experts
    )
    rows = with_weights(hidden_states.reshape(total, feature_width), weights)
    outputs = []
    for piece in range(PIECES):
        near = rows[piece * share : (piece + 1) * share]
        for bit in bits[:-1]:
            near = jnp.concatenate([near, swap(near, axis_size, bit)], axis=0)
        far = swap(near, axis_size, bits[-1])
        keep, send = expert_rows(near, far, experts, gate_proj[0], up_proj[0], down_proj[0])
        for bit in reversed(bits[1:]):
            keep, send = add_halves(keep, swap(send, axis_size, bit))
        arrived = swap(send, axis_size, bits[0])
        outputs.append((keep.astype(jnp.float32) + arrived.astype(jnp.float32)).astype(jnp.bfloat16))
    return jnp.concatenate(outputs, axis=0).reshape(hidden_states.shape)


def solution(mesh):
    placed = (
        P(None, ("groups", "expert"), None),
        P(None, ("groups", "expert"), None),
        P(None, ("groups", "expert"), None),
        P("expert", None, None),
        P("expert", None, None),
        P("expert", None, None),
    )
    return jax.shard_map(
        on_device,
        mesh=mesh,
        in_specs=placed,
        out_specs=P(None, ("groups", "expert"), None),
        check_vma=False,
    )
```

```python
import jax
import jax.numpy as jnp
from jax import lax
from jax.experimental import pallas as pl
from jax.experimental.pallas import tpu as pltpu
from jax.sharding import PartitionSpec as P

PIECES = 4
LANES = 128
BLOCK = 256
MIB = 1024 * 1024
WORK_COST = pl.CostEstimate(flops=1000, bytes_accessed=1000, transcendentals=0)
VMEM = pl.BlockSpec(memory_space=pltpu.VMEM)


def swap(array, axis_size, bit):
    return lax.ppermute(array, "expert", [(i, i ^ bit) for i in range(axis_size)])


def after(array, *others):
    return lax.optimization_barrier((array, *others))[0]


def prepare_kernel(experts, rows_ref, ids_ref, weights_ref, *refs):
    piece_refs, (ids_held, weights_held, sems) = refs[:-3], refs[-3:]
    steps, _, row_count = ids_ref.shape
    width = rows_ref.shape[1]
    share, full = piece_refs[0].shape
    small = [
        pltpu.make_async_copy(ids_ref, ids_held, sems.at[0]),
        pltpu.make_async_copy(weights_ref, weights_held, sems.at[1]),
    ]
    large = [
        pltpu.make_async_copy(
            rows_ref.at[pl.ds(piece * share, share)],
            ref.at[:, pl.ds(0, width)],
            sems.at[2 + piece],
        )
        for piece, ref in enumerate(piece_refs)
    ]
    for copy in small + large:
        copy.start()
    for copy in small:
        copy.wait()
    columns = []
    for step in range(steps):
        ids, weights = ids_held[step], weights_held[step]
        normalized = weights / jnp.sum(weights, axis=0, keepdims=True)
        labels = lax.broadcasted_iota(jnp.int32, (experts, row_count), 0)
        spread = jnp.zeros((experts, row_count), jnp.float32)
        for choice in range(ids.shape[0]):
            mine = ids[choice : choice + 1, :] == labels
            spread = spread + jnp.where(mine, normalized[choice : choice + 1, :], 0.0)
        high = spread.astype(jnp.bfloat16)
        low = (spread - high.astype(jnp.float32)).astype(jnp.bfloat16)
        parts = jnp.concatenate([high, low], axis=0)
        line = lax.broadcasted_iota(jnp.int32, (2 * experts, full - width), 0)
        lane = lax.broadcasted_iota(jnp.int32, (2 * experts, full - width), 1)
        unit = (line == lane).astype(jnp.bfloat16)
        turned = lax.dot_general(
            parts, unit, (((0,), (0,)), ((), ())), preferred_element_type=jnp.float32
        )
        columns.append(turned.astype(jnp.bfloat16))
    column = jnp.concatenate(columns, axis=0)
    for piece, ref in enumerate(piece_refs):
        ref[:, width:] = column[piece * share : (piece + 1) * share]
    for copy in large:
        copy.wait()


def prepare(rows, route_ids, route_weights, experts):
    total, width = rows.shape
    full = width + -(-2 * experts // LANES) * LANES
    shape = jax.ShapeDtypeStruct((total // PIECES, full), rows.dtype)
    ids, weights = jnp.swapaxes(route_ids, 1, 2), jnp.swapaxes(route_weights, 1, 2)
    return pl.pallas_call(
        lambda *refs: prepare_kernel(experts, *refs),
        out_shape=(shape,) * PIECES,
        in_specs=[pl.BlockSpec(memory_space=pltpu.HBM)] * 3,
        out_specs=(VMEM,) * PIECES,
        scratch_shapes=[
            pltpu.VMEM(ids.shape, ids.dtype),
            pltpu.VMEM(weights.shape, weights.dtype),
            pltpu.SemaphoreType.DMA((2 + PIECES,)),
        ],
        compiler_params=pltpu.CompilerParams(vmem_limit_bytes=40 * MIB),
    )(rows, ids, weights)


def expert_kernel(experts, places, own_ref, near_ref, far_ref, gate_ref, up_ref, down_ref, keep_ref, send_ref):
    width = gate_ref.shape[0]
    half = near_ref.shape[0]
    share = half // len(places)
    own = own_ref[0]
    block = min(BLOCK // 2, half)
    for start in range(0, half, block):
        part = slice(start, start + block)
        rows = jnp.concatenate([near_ref[part, :], far_ref[part, :]], axis=0)
        tokens = rows[:, :width]
        spread = rows[:, width:].astype(jnp.float32)
        lane = lax.broadcasted_iota(jnp.int32, spread.shape, 1)
        mine = (lane == own) | (lane == own + experts)
        weight = jnp.sum(jnp.where(mine, spread, 0.0), axis=1, keepdims=True)
        gate = jnp.dot(tokens, gate_ref[...], preferred_element_type=jnp.float32)
        up = jnp.dot(tokens, up_ref[...], preferred_element_type=jnp.float32)
        hidden = (gate / (1.0 + jnp.exp(-gate)) * up).astype(jnp.bfloat16)
        result = jnp.dot(hidden, down_ref[...], preferred_element_type=jnp.float32)
        scaled = (result * weight).astype(jnp.bfloat16)
        for row in range(0, block, share):
            place = places[(start + row) // share] * share
            keep_ref[place : place + share, :] = scaled[row : row + share]
            send_ref[place : place + share, :] = scaled[block + row : block + row + share]


def places_of(gather, scatter):
    blocks = []
    for index in range(1 << (len(gather) - 1)):
        taken = {bit for place, bit in enumerate(gather[:-1]) if index >> place & 1}
        blocks.append(sum(1 << place for place, bit in enumerate(reversed(scatter[1:])) if bit in taken))
    return tuple(blocks)


def expert_rows(near, far, experts, places, gate_proj, up_proj, down_proj):
    half = near.shape[0]
    shape = jax.ShapeDtypeStruct((half, gate_proj.shape[0]), jnp.bfloat16)
    return pl.pallas_call(
        lambda *refs: expert_kernel(experts, places, *refs),
        out_shape=(shape, shape),
        in_specs=[pl.BlockSpec(memory_space=pltpu.SMEM)] + [VMEM] * 5,
        out_specs=(VMEM, VMEM),
        compiler_params=pltpu.CompilerParams(vmem_limit_bytes=32 * MIB),
        cost_estimate=WORK_COST,
    )(lax.axis_index("expert").reshape(1), near, far, gate_proj, up_proj, down_proj)


def total_of(first, second):
    return (first.astype(jnp.float32) + second.astype(jnp.float32)).astype(jnp.bfloat16)


def add_halves(kept, arrived):
    half = kept.shape[0] // 2
    return total_of(kept[:half], arrived[:half]), total_of(kept[half:], arrived[half:])


def on_device(hidden_states, route_ids, route_weights, gate_proj, up_proj, down_proj):
    step_count, row_count, feature_width = hidden_states.shape
    axis_size = lax.axis_size("expert")
    experts = axis_size * gate_proj.shape[0]
    bits = [1 << i for i in reversed(range(axis_size.bit_length() - 1))]
    beside, last = bits[-2:]
    outward = bits
    gathers = [outward] * PIECES
    scatters = [outward[::-1]] * PIECES

    rows = hidden_states.reshape(step_count * row_count, feature_width)
    pieces = prepare(rows, route_ids, route_weights, experts)
    matrices = gate_proj[0], up_proj[0], down_proj[0]
    held = list(pieces)
    got = {}

    def grow(piece, stage, *ties, late=()):
        bit = gathers[piece][stage]
        far = swap(after(held[piece], *ties) if ties else held[piece], axis_size, bit)
        own = after(held[piece], *late) if late else held[piece]
        held[piece] = jnp.concatenate([own, far], axis=0)
        got[piece, stage] = held[piece]

    final = len(bits) - 1
    for piece in range(PIECES):
        ties = () if piece == 0 else (got[0, 0],) if piece == 1 else (got[piece - 2, final - 2],)
        grow(piece, 0, *ties)
        for stage in range(1, final):
            grow(piece, stage)
    sums = []
    for piece in range(PIECES):
        near = after(held[piece], sums[-1][0]) if sums else held[piece]
        far = swap(near, axis_size, last)
        places = places_of(gathers[piece], scatters[piece])
        sums.append(expert_rows(near, far, experts, places, *matrices))

    def shrink(piece, stage, *late):
        keep, send = sums[piece]
        if late:
            keep = after(keep, *late)
        arrived = swap(send, axis_size, scatters[piece][stage])
        if stage == final:
            sums[piece] = (total_of(keep, arrived), None)
        else:
            sums[piece] = add_halves(keep, arrived)

    firsts = [keep for keep, _ in sums]
    for piece in range(PIECES):
        shrink(piece, 0, *firsts[piece + 1 : piece + 2])
    closed = sums[-1][0]

    for stage in range(1, final + 1):
        for piece in range(PIECES):
            shrink(piece, stage, *((closed,) if stage == 1 and piece + 1 < PIECES else ()))
    outputs = [total for total, _ in sums]
    return jnp.concatenate(outputs, axis=0).reshape(hidden_states.shape)


def solution(mesh):
    placed = (
        P(None, ("groups", "expert"), None),
        P(None, ("groups", "expert"), None),
        P(None, ("groups", "expert"), None),
        P("expert", None, None),
        P("expert", None, None),
        P("expert", None, None),
    )
    return jax.shard_map(
        on_device,
        mesh=mesh,
        in_specs=placed,
        out_specs=P(None, ("groups", "expert"), None),
        check_vma=False,
    )
```

```python
import jax
import jax.numpy as jnp
from jax import lax
from jax.experimental import pallas as pl
from jax.experimental.pallas import tpu as pltpu
from jax.sharding import PartitionSpec as P

PIECES = 4
LANES = 128
BLOCK = 256
MIB = 1024 * 1024
WORK_COST = pl.CostEstimate(flops=1000, bytes_accessed=1000, transcendentals=0)
VMEM = pl.BlockSpec(memory_space=pltpu.VMEM)


def swap(array, axis_size, bit):
    return lax.ppermute(array, "expert", [(i, i ^ bit) for i in range(axis_size)])


def after(array, *others):
    return lax.optimization_barrier((array, *others))[0]


def prepare_kernel(experts, rows_ref, ids_ref, weights_ref, *refs):
    piece_refs, (ids_held, weights_held, sems) = refs[:-3], refs[-3:]
    steps, _, row_count = ids_ref.shape
    width = rows_ref.shape[1]
    share, full = piece_refs[0].shape
    small = [
        pltpu.make_async_copy(ids_ref, ids_held, sems.at[0]),
        pltpu.make_async_copy(weights_ref, weights_held, sems.at[1]),
    ]
    large = [
        pltpu.make_async_copy(
            rows_ref.at[pl.ds(piece * share, share)],
            ref.at[:, pl.ds(0, width)],
            sems.at[2 + piece],
        )
        for piece, ref in enumerate(piece_refs)
    ]
    for copy in small + large:
        copy.start()
    for copy in small:
        copy.wait()
    columns = []
    for step in range(steps):
        ids, weights = ids_held[step], weights_held[step]
        normalized = weights / jnp.sum(weights, axis=0, keepdims=True)
        labels = lax.broadcasted_iota(jnp.int32, (experts, row_count), 0)
        spread = jnp.zeros((experts, row_count), jnp.float32)
        for choice in range(ids.shape[0]):
            mine = ids[choice : choice + 1, :] == labels
            spread = spread + jnp.where(mine, normalized[choice : choice + 1, :], 0.0)
        high = spread.astype(jnp.bfloat16)
        low = (spread - high.astype(jnp.float32)).astype(jnp.bfloat16)
        parts = jnp.concatenate([high, low], axis=0)
        line = lax.broadcasted_iota(jnp.int32, (2 * experts, full - width), 0)
        lane = lax.broadcasted_iota(jnp.int32, (2 * experts, full - width), 1)
        unit = (line == lane).astype(jnp.bfloat16)
        turned = lax.dot_general(
            parts, unit, (((0,), (0,)), ((), ())), preferred_element_type=jnp.float32
        )
        columns.append(turned.astype(jnp.bfloat16))
    column = jnp.concatenate(columns, axis=0)
    for piece, ref in enumerate(piece_refs):
        ref[:, width:] = column[piece * share : (piece + 1) * share]
    for copy in large:
        copy.wait()


def prepare(rows, route_ids, route_weights, experts):
    total, width = rows.shape
    full = width + -(-2 * experts // LANES) * LANES
    shape = jax.ShapeDtypeStruct((total // PIECES, full), rows.dtype)
    ids, weights = jnp.swapaxes(route_ids, 1, 2), jnp.swapaxes(route_weights, 1, 2)
    return pl.pallas_call(
        lambda *refs: prepare_kernel(experts, *refs),
        out_shape=(shape,) * PIECES,
        in_specs=[pl.BlockSpec(memory_space=pltpu.HBM)] * 3,
        out_specs=(VMEM,) * PIECES,
        scratch_shapes=[
            pltpu.VMEM(ids.shape, ids.dtype),
            pltpu.VMEM(weights.shape, weights.dtype),
            pltpu.SemaphoreType.DMA((2 + PIECES,)),
        ],
        compiler_params=pltpu.CompilerParams(vmem_limit_bytes=40 * MIB),
    )(rows, ids, weights)


def expert_kernel(experts, places, own_ref, near_ref, far_ref, gate_ref, up_ref, down_ref, keep_ref, send_ref):
    width = gate_ref.shape[0]
    half = near_ref.shape[0]
    share = half // len(places)
    own = own_ref[0]
    block = min(BLOCK // 2, half)
    for start in range(0, half, block):
        part = slice(start, start + block)
        rows = jnp.concatenate([near_ref[part, :], far_ref[part, :]], axis=0)
        tokens = rows[:, :width]
        spread = rows[:, width:].astype(jnp.float32)
        lane = lax.broadcasted_iota(jnp.int32, spread.shape, 1)
        mine = (lane == own) | (lane == own + experts)
        weight = jnp.sum(jnp.where(mine, spread, 0.0), axis=1, keepdims=True)
        gate = jnp.dot(tokens, gate_ref[...], preferred_element_type=jnp.float32)
        up = jnp.dot(tokens, up_ref[...], preferred_element_type=jnp.float32)
        hidden = (gate / (1.0 + jnp.exp(-gate)) * up).astype(jnp.bfloat16)
        result = jnp.dot(hidden, down_ref[...], preferred_element_type=jnp.float32)
        scaled = (result * weight).astype(jnp.bfloat16)
        for row in range(0, block, share):
            place = places[(start + row) // share] * share
            keep_ref[place : place + share, :] = scaled[row : row + share]
            send_ref[place : place + share, :] = scaled[block + row : block + row + share]


def places_of(gather, scatter):
    blocks = []
    for index in range(1 << (len(gather) - 1)):
        taken = {bit for place, bit in enumerate(gather[:-1]) if index >> place & 1}
        blocks.append(sum(1 << place for place, bit in enumerate(reversed(scatter[1:])) if bit in taken))
    return tuple(blocks)


def expert_rows(near, far, experts, places, gate_proj, up_proj, down_proj):
    half = near.shape[0]
    shape = jax.ShapeDtypeStruct((half, gate_proj.shape[0]), jnp.bfloat16)
    return pl.pallas_call(
        lambda *refs: expert_kernel(experts, places, *refs),
        out_shape=(shape, shape),
        in_specs=[pl.BlockSpec(memory_space=pltpu.SMEM)] + [VMEM] * 5,
        out_specs=(VMEM, VMEM),
        compiler_params=pltpu.CompilerParams(vmem_limit_bytes=32 * MIB),
        cost_estimate=WORK_COST,
    )(lax.axis_index("expert").reshape(1), near, far, gate_proj, up_proj, down_proj)


def total_of(first, second):
    return (first.astype(jnp.float32) + second.astype(jnp.float32)).astype(jnp.bfloat16)


def add_halves(kept, arrived):
    half = kept.shape[0] // 2
    return total_of(kept[:half], arrived[:half]), total_of(kept[half:], arrived[half:])


def on_device(hidden_states, route_ids, route_weights, gate_proj, up_proj, down_proj):
    step_count, row_count, feature_width = hidden_states.shape
    axis_size = lax.axis_size("expert")
    experts = axis_size * gate_proj.shape[0]
    bits = [1 << i for i in reversed(range(axis_size.bit_length() - 1))]
    beside, last = bits[-2:]
    outward = bits
    early = [beside] + bits[:-2] + [last]
    gathers = [outward] * (PIECES - 1) + [early]
    scatters = [outward[::-1]] * PIECES

    rows = hidden_states.reshape(step_count * row_count, feature_width)
    pieces = prepare(rows, route_ids, route_weights, experts)
    matrices = gate_proj[0], up_proj[0], down_proj[0]
    held = list(pieces)
    got = {}

    def grow(piece, stage, *ties, late=()):
        bit = gathers[piece][stage]
        far = swap(after(held[piece], *ties) if ties else held[piece], axis_size, bit)
        own = after(held[piece], *late) if late else held[piece]
        held[piece] = jnp.concatenate([own, far], axis=0)
        got[piece, stage] = held[piece]

    final = len(bits) - 1
    sums, crossed = [None] * PIECES, {}

    def cross(piece, *ties):
        near = after(held[piece], *ties) if ties else held[piece]
        crossed[piece] = near, swap(near, axis_size, last)

    def work(piece, *late):
        near, far = crossed[piece]
        near = after(near, *late) if late else near
        sums[piece] = expert_rows(near, far, experts, places_of(gathers[piece], scatters[piece]), *matrices)

    for piece in (0, 1):
        for stage in range(final):
            grow(piece, stage, *((got[0, 0],) if (piece, stage) == (1, 0) else ()))
    grow(PIECES - 1, 0)

    grow(2, 0, got[0, final - 2])
    for stage in range(1, final):
        grow(2, stage)
    for stage in range(1, final):
        grow(3, stage, *((got[1, final - 2],) if stage == 1 else ()))
    for piece in range(PIECES):
        cross(piece, *((sums[piece - 2][0],) if piece >= 2 else ()))
        work(piece)

    def shrink(piece, stage, *late):
        keep, send = sums[piece]
        if late:
            keep = after(keep, *late)
        arrived = swap(send, axis_size, scatters[piece][stage])
        if stage == final:
            sums[piece] = (total_of(keep, arrived), None)
        else:
            sums[piece] = add_halves(keep, arrived)

    firsts = [keep for keep, _ in sums]
    for piece in range(PIECES):
        shrink(piece, 0, *firsts[piece + 1 : piece + 2])
    closed = sums[-1][0]

    for stage in range(1, final + 1):
        for piece in range(PIECES):
            shrink(piece, stage, *((closed,) if stage == 1 and piece + 1 < PIECES else ()))
    outputs = [total for total, _ in sums]
    return jnp.concatenate(outputs, axis=0).reshape(hidden_states.shape)


def solution(mesh):
    placed = (
        P(None, ("groups", "expert"), None),
        P(None, ("groups", "expert"), None),
        P(None, ("groups", "expert"), None),
        P("expert", None, None),
        P("expert", None, None),
        P("expert", None, None),
    )
    return jax.shard_map(
        on_device,
        mesh=mesh,
        in_specs=placed,
        out_specs=P(None, ("groups", "expert"), None),
        check_vma=False,
    )
```

```python
import jax
import jax.numpy as jnp
from jax import lax
from jax.experimental import pallas as pl
from jax.experimental.pallas import tpu as pltpu
from jax.sharding import PartitionSpec as P

PIECES = 4
LANES = 128
BLOCK = 256
MIB = 1024 * 1024
WORK_COST = pl.CostEstimate(flops=1000, bytes_accessed=1000, transcendentals=0)
VMEM = pl.BlockSpec(memory_space=pltpu.VMEM)


def swap(array, axis_size, bit):
    return lax.ppermute(array, "expert", [(i, i ^ bit) for i in range(axis_size)])


def after(array, *others):
    return lax.optimization_barrier((array, *others))[0]


def prepare_kernel(experts, rows_ref, ids_ref, weights_ref, *refs):
    piece_refs, (ids_held, weights_held, sems) = refs[:-3], refs[-3:]
    steps, _, row_count = ids_ref.shape
    width = rows_ref.shape[1]
    share, full = piece_refs[0].shape
    small = [
        pltpu.make_async_copy(ids_ref, ids_held, sems.at[0]),
        pltpu.make_async_copy(weights_ref, weights_held, sems.at[1]),
    ]
    large = [
        pltpu.make_async_copy(
            rows_ref.at[pl.ds(piece * share, share)],
            ref.at[:, pl.ds(0, width)],
            sems.at[2 + piece],
        )
        for piece, ref in enumerate(piece_refs)
    ]
    for copy in small + large:
        copy.start()
    for copy in small:
        copy.wait()
    columns = []
    for step in range(steps):
        ids, weights = ids_held[step], weights_held[step]
        normalized = weights / jnp.sum(weights, axis=0, keepdims=True)
        labels = lax.broadcasted_iota(jnp.int32, (experts, row_count), 0)
        spread = jnp.zeros((experts, row_count), jnp.float32)
        for choice in range(ids.shape[0]):
            mine = ids[choice : choice + 1, :] == labels
            spread = spread + jnp.where(mine, normalized[choice : choice + 1, :], 0.0)
        high = spread.astype(jnp.bfloat16)
        low = (spread - high.astype(jnp.float32)).astype(jnp.bfloat16)
        parts = jnp.concatenate([high, low], axis=0)
        line = lax.broadcasted_iota(jnp.int32, (2 * experts, full - width), 0)
        lane = lax.broadcasted_iota(jnp.int32, (2 * experts, full - width), 1)
        unit = (line == lane).astype(jnp.bfloat16)
        turned = lax.dot_general(
            parts, unit, (((0,), (0,)), ((), ())), preferred_element_type=jnp.float32
        )
        columns.append(turned.astype(jnp.bfloat16))
    column = jnp.concatenate(columns, axis=0)
    for piece, ref in enumerate(piece_refs):
        ref[:, width:] = column[piece * share : (piece + 1) * share]
    for copy in large:
        copy.wait()


def prepare(rows, route_ids, route_weights, experts):
    total, width = rows.shape
    full = width + -(-2 * experts // LANES) * LANES
    shape = jax.ShapeDtypeStruct((total // PIECES, full), rows.dtype)
    ids, weights = jnp.swapaxes(route_ids, 1, 2), jnp.swapaxes(route_weights, 1, 2)
    return pl.pallas_call(
        lambda *refs: prepare_kernel(experts, *refs),
        out_shape=(shape,) * PIECES,
        in_specs=[pl.BlockSpec(memory_space=pltpu.HBM)] * 3,
        out_specs=(VMEM,) * PIECES,
        scratch_shapes=[
            pltpu.VMEM(ids.shape, ids.dtype),
            pltpu.VMEM(weights.shape, weights.dtype),
            pltpu.SemaphoreType.DMA((2 + PIECES,)),
        ],
        compiler_params=pltpu.CompilerParams(vmem_limit_bytes=40 * MIB),
    )(rows, ids, weights)


def expert_kernel(experts, places, own_ref, near_ref, far_ref, gate_ref, up_ref, down_ref, keep_ref, send_ref, rows_ref, hidden_ref):
    width = gate_ref.shape[0]
    half = near_ref.shape[0]
    share = half // len(places)
    own = own_ref[0]
    block = min(BLOCK // 2, half)
    for start in range(0, half, block):
        part = slice(start, start + block)
        rows_ref[:block, :] = near_ref[part, :]
        rows_ref[block:, :] = far_ref[part, :]
        spread = rows_ref[:, width:].astype(jnp.float32)
        lane = lax.broadcasted_iota(jnp.int32, spread.shape, 1)
        mine = (lane == own) | (lane == own + experts)
        weight = jnp.sum(jnp.where(mine, spread, 0.0), axis=1, keepdims=True)
        for begin in range(0, hidden_ref.shape[1], BLOCK):
            cut = slice(begin, begin + BLOCK)
            gate = jnp.dot(rows_ref[:, :width], gate_ref[:, cut], preferred_element_type=jnp.float32)
            up = jnp.dot(rows_ref[:, :width], up_ref[:, cut], preferred_element_type=jnp.float32)
            hidden_ref[:, cut] = (gate / (1.0 + jnp.exp(-gate)) * up).astype(jnp.bfloat16)
        for begin in range(0, width, width):
            cut = slice(begin, begin + width)
            result = jnp.dot(hidden_ref[...], down_ref[:, cut], preferred_element_type=jnp.float32)
            scaled = (result * weight).astype(jnp.bfloat16)
            for row in range(0, block, share):
                place = places[(start + row) // share] * share
                keep_ref[place : place + share, cut] = scaled[row : row + share]
                send_ref[place : place + share, cut] = scaled[block + row : block + row + share]


def places_of(gather, scatter):
    blocks = []
    for index in range(1 << (len(gather) - 1)):
        taken = {bit for place, bit in enumerate(gather[:-1]) if index >> place & 1}
        blocks.append(sum(1 << place for place, bit in enumerate(reversed(scatter[1:])) if bit in taken))
    return tuple(blocks)


def expert_rows(near, far, experts, places, gate_proj, up_proj, down_proj):
    half = near.shape[0]
    shape = jax.ShapeDtypeStruct((half, gate_proj.shape[0]), jnp.bfloat16)
    return pl.pallas_call(
        lambda *refs: expert_kernel(experts, places, *refs),
        out_shape=(shape, shape),
        in_specs=[pl.BlockSpec(memory_space=pltpu.SMEM)] + [VMEM] * 5,
        out_specs=(VMEM, VMEM),
        scratch_shapes=[
            pltpu.VMEM((2 * min(BLOCK // 2, half), near.shape[1]), jnp.bfloat16),
            pltpu.VMEM((2 * min(BLOCK // 2, half), gate_proj.shape[1]), jnp.bfloat16),
        ],
        compiler_params=pltpu.CompilerParams(vmem_limit_bytes=32 * MIB),
        cost_estimate=WORK_COST,
    )(lax.axis_index("expert").reshape(1), near, far, gate_proj, up_proj, down_proj)


def total_of(first, second):
    return (first.astype(jnp.float32) + second.astype(jnp.float32)).astype(jnp.bfloat16)


def add_halves(kept, arrived):
    half = kept.shape[0] // 2
    return total_of(kept[:half], arrived[:half]), total_of(kept[half:], arrived[half:])


def on_device(hidden_states, route_ids, route_weights, gate_proj, up_proj, down_proj):
    step_count, row_count, feature_width = hidden_states.shape
    axis_size = lax.axis_size("expert")
    experts = axis_size * gate_proj.shape[0]
    bits = [1 << i for i in reversed(range(axis_size.bit_length() - 1))]
    beside, last = bits[-2:]
    outward = bits
    early = [beside] + bits[:-2] + [last]
    gathers = [outward] * (PIECES - 1) + [early]
    scatters = [outward[::-1]] * PIECES

    rows = hidden_states.reshape(step_count * row_count, feature_width)
    pieces = prepare(rows, route_ids, route_weights, experts)
    matrices = gate_proj[0], up_proj[0], down_proj[0]
    held = list(pieces)
    got = {}

    def grow(piece, stage, *ties, late=()):
        bit = gathers[piece][stage]
        far = swap(after(held[piece], *ties) if ties else held[piece], axis_size, bit)
        own = after(held[piece], *late) if late else held[piece]
        held[piece] = jnp.concatenate([own, far], axis=0)
        got[piece, stage] = held[piece]

    final = len(bits) - 1
    sums, crossed = [None] * PIECES, {}

    def cross(piece, *ties):
        near = after(held[piece], *ties) if ties else held[piece]
        crossed[piece] = near, swap(near, axis_size, last)

    def work(piece, *late):
        near, far = crossed[piece]
        near = after(near, *late) if late else near
        sums[piece] = expert_rows(near, far, experts, places_of(gathers[piece], scatters[piece]), *matrices)

    for piece in (0, 1):
        for stage in range(final):
            grow(piece, stage, *((got[0, 0],) if (piece, stage) == (1, 0) else ()))
    grow(PIECES - 1, 0)

    grow(2, 0, got[0, final - 2])
    for stage in range(1, final):
        grow(2, stage)
    for stage in range(1, final):
        grow(3, stage, *((got[1, final - 2],) if stage == 1 else ()))
    for piece in range(PIECES):
        cross(piece, *((sums[piece - 2][0],) if piece >= 2 else ()))
        work(piece)

    def shrink(piece, stage, *late):
        keep, send = sums[piece]
        if late:
            keep = after(keep, *late)
        arrived = swap(send, axis_size, scatters[piece][stage])
        if stage == final:
            sums[piece] = (total_of(keep, arrived), None)
        else:
            sums[piece] = add_halves(keep, arrived)

    firsts = [keep for keep, _ in sums]
    for piece in range(PIECES):
        shrink(piece, 0, *firsts[piece + 1 : piece + 2] if piece else ())
    closed = sums[-1][0]

    for stage in range(1, final + 1):
        for piece in range(PIECES):
            shrink(piece, stage, *((closed,) if stage == 1 and piece + 1 < PIECES else ()))
    outputs = [total for total, _ in sums]
    return jnp.concatenate(outputs, axis=0).reshape(hidden_states.shape)


def solution(mesh):
    placed = (
        P(None, ("groups", "expert"), None),
        P(None, ("groups", "expert"), None),
        P(None, ("groups", "expert"), None),
        P("expert", None, None),
        P("expert", None, None),
        P("expert", None, None),
    )
    return jax.shard_map(
        on_device,
        mesh=mesh,
        in_specs=placed,
        out_specs=P(None, ("groups", "expert"), None),
        check_vma=False,
    )
```
